32 devices in a mesh: ctx: 8 (over y, x, core), tp: 4 (over z).
Axes of the slice: x: 2, y: 2, z: 4, core: 2. Of those that a mesh axis runs over, the one named last changes fastest.
Arguments:
- query_feat: bfloat16 [8192, 8192], P('tp', 'ctx'), may hold values from -6 to 6
- key_feat: bfloat16 [8192, 8192], P('tp', 'ctx'), may hold values from -6 to 6
- value_feat: bfloat16 [8192, 8192], P('tp', 'ctx'), may hold values from -6 to 6
- short_filter: float32 [3, 3, 8192], P(None, None, 'tp'), may hold values from -3 to 3
- skip: float32 [8192], P('tp'), may hold values from -3 to 3
- decay_rate: float32 [64, 16], P('tp'), may hold values from 2.4414063e-05 to 0.04, as said below
- residue: float32 [64, 16], P('tp'), may hold values from -1 to 1
Outputs:
- regrouped: bfloat16 [64, 128, 8192], P('ctx', 'tp')
The draws below stay inside these ranges and needn't reach their ends.
Inputs may be any that keep to these rules, and one draw needn't show every extreme that they name: `decay_rate`: positive decay rates of the modes.
All inputs are finite; a program needn't handle non-finite values.
Results may differ from the reference program's by a relative error of at most 0.001.
Values may be sent and summed in bfloat16 or wider, within the bound.
A program may use at most 128 MiB of HBM per device.

```python
import math
import jax
import jax.numpy as jnp
from jax import lax

HEADS = 64
HEAD_DIM = 128
MODES = 16
TOK_DEV = 1024
D = 8192
TOKENS = 8192


def mode_table(key):
    base = jax.random.fold_in(key, 11)
    first, second, third, fourth = jax.random.split(base, 4)
    shape = (HEADS, MODES)
    slow_share = 0.5
    chosen = jax.random.uniform(first, shape) < slow_share
    slow = jnp.exp(jax.random.uniform(second, shape, minval=math.log(0.2), maxval=math.log(2.0))) / TOKENS
    fast = jnp.exp(jax.random.uniform(third, shape, minval=math.log(1.0 / 200.0), maxval=math.log(1.0 / 25.0)))
    rate = jnp.where(chosen, slow, fast).astype(jnp.float32)
    amplitude = jnp.clip(jax.random.normal(fourth, shape), -5.0, 5.0) * 0.7
    weight = (amplitude * jnp.sqrt(rate)).astype(jnp.float32)
    return (rate, weight)


def draw_decay_rate(key, part):
    return mode_table(key)[0]


def draw_residue(key, part):
    return mode_table(key)[1]


def block_scale(key, dims, pieces, low, largest):
    gain, own = 1.0, jax.random.fold_in(key, 6)
    for position, parts in pieces:
        draws = jnp.exp(jax.random.uniform(jax.random.fold_in(own, position), (parts,), jnp.float32, low / len(pieces), largest / len(pieces)))
        gain = gain * jnp.repeat(draws, dims[position] // parts).reshape([-1 if axis == position else 1 for axis in range(len(dims))])
    return gain


def gaussian(key, extent, scale, reach, cuts=(), held_as=jnp.bfloat16):
    values = jax.random.normal(key, extent, jnp.float32) * scale
    if len(cuts) > 0:
        values = block_scale(key, extent, cuts, -0.22, 0.18) * values
    return jnp.clip(values, min=-reach, max=reach).astype(held_as)


def setup_inputs(seed: int = 0) -> dict:
    key_of = jax.random.split(jax.random.key(seed), 8)
    return {
        "query_feat": gaussian(key_of[0], (D, TOKENS), 1.0, 6.0, ((0, 4), (1, 8))),
        "key_feat": gaussian(key_of[1], (D, TOKENS), 1.0, 6.0, ((0, 4), (1, 8))),
        "value_feat": gaussian(key_of[2], (D, TOKENS), 1.0, 6.0, ((0, 4), (1, 8))),
        "short_filter": gaussian(key_of[3], (3, 3, D), 0.5, 3.0, ((2, 4),), jnp.float32),
        "skip": gaussian(key_of[4], (D,), 0.5, 3.0, ((0, 4),), jnp.float32),
        "decay_rate": draw_decay_rate(jax.random.fold_in(key_of[7], 71), 0),
        "residue": draw_residue(jax.random.fold_in(key_of[7], 71), 0),
    }


def short_conv(features, taps):
    padded = jnp.pad(features, ((0, 0), (2, 0)))
    count = features.shape[1]
    return taps[0][:, None] * padded[:, 2:] + taps[1][:, None] * padded[:, 1:count + 1] + taps[2][:, None] * padded[:, :count]


def mix_head(inputs):
    query_h, key_h, value_h, taps, skip_h, rate, weight = inputs
    query_s = short_conv(query_h.astype(jnp.float32), taps[0])
    key_s = short_conv(key_h.astype(jnp.float32), taps[1])
    value_s = short_conv(value_h.astype(jnp.float32), taps[2])
    products = key_s * value_s
    channels = products.shape[0]
    blocks = products.shape[1] // TOK_DEV
    width = TOK_DEV
    prod_blocks = products.reshape(channels, blocks, width).transpose(1, 0, 2)
    gate_blocks = query_s.reshape(channels, blocks, width).transpose(1, 0, 2)
    lag = jnp.arange(width).astype(jnp.float32)
    filt = jnp.sum(weight[:, None] * jnp.exp(-rate[:, None] * lag[None, :]), axis=0)
    offset = jnp.arange(width)[:, None] - jnp.arange(width)[None, :]
    toeplitz = jnp.where(offset >= 0, filt[jnp.clip(offset, 0, width - 1)], jnp.float32(0.0))
    near = jnp.einsum('bcs,ts->bct', prod_blocks, toeplitz, precision=lax.Precision.HIGHEST)
    to_end = jnp.exp(-rate[:, None] * (width - 1.0 - lag)[None, :])
    states = jnp.einsum('ns,bcs->bnc', to_end, prod_blocks, precision=lax.Precision.HIGHEST)
    carry_decay = jnp.exp(-rate * width)

    def advance(state, block_state):
        return carry_decay[:, None] * state + block_state, state

    _, entering = lax.scan(advance, jnp.zeros((rate.shape[0], channels), jnp.float32), states)
    from_start = weight[None, :] * jnp.exp(-rate[None, :] * (lag[:, None] + 1.0))
    far = jnp.einsum('tn,bnc->bct', from_start, entering, precision=lax.Precision.HIGHEST)
    gated = gate_blocks * (near + far + skip_h[None, :, None] * prod_blocks)
    return gated.transpose(1, 0, 2).reshape(channels, blocks * width).astype(jnp.bfloat16)


def reference(query_feat, key_feat, value_feat, short_filter, skip, decay_rate, residue):
    total = query_feat.shape[1]
    query_h = query_feat.reshape(HEADS, HEAD_DIM, total)
    key_h = key_feat.reshape(HEADS, HEAD_DIM, total)
    value_h = value_feat.reshape(HEADS, HEAD_DIM, total)
    taps = short_filter.reshape(3, 3, HEADS, HEAD_DIM).transpose(2, 0, 1, 3)
    skip_h = skip.reshape(HEADS, HEAD_DIM)
    return lax.map(mix_head, (query_h, key_h, value_h, taps, skip_h, decay_rate, residue))
```

```python
import functools

import jax
import jax.numpy as jnp
from jax import lax
from jax.experimental import pallas as pl
from jax.experimental.pallas import tpu as pltpu
from jax.sharding import PartitionSpec as P

LANES = 128
MESH = pl.DeviceIdType.MESH
F32 = jnp.float32
BF16 = jnp.bfloat16


def split2(x):
    high = x.astype(BF16).astype(F32)
    return high, x - high


def kernel(
    size, q_hbm, k_hbm, v_hbm, cols, rate_row, rate_col, weight_col, out,
    qbuf, kbuf, vbuf, halo, phi, plo, acc, sbuf, rbuf, chunk_states, own_states, got_states,
    in_sem, halo_send, halo_recv, st_send, st_recv, a_send, a_recv, b_send, b_recv,
):
    n_ctx, n_tp, heads, hd, width, modes, chunk, group = size
    c = lax.axis_index("ctx")
    z = lax.axis_index("tp")
    ng = heads // group
    rows_g = group * hd
    ratio = n_ctx // n_tp
    heads_out = heads // ratio
    ngo = heads_out // group
    part = hd // n_tp
    nch = width // chunk
    hbms = (k_hbm, v_hbm, q_hbm)
    bufs = (kbuf, vbuf, qbuf)

    def load(f, g):
        rows = pl.ds(pl.multiple_of(g * rows_g, rows_g), rows_g)
        return pltpu.make_async_copy(hbms[f].at[rows], bufs[f].at[rows], in_sem.at[f, g])

    def send_halo(f, g):
        rows = pl.ds(pl.multiple_of(g * rows_g, rows_g), rows_g)
        return pltpu.make_async_remote_copy(
            src_ref=hbms[f].at[rows, pl.ds(width - LANES, LANES)],
            dst_ref=halo.at[f, rows],
            send_sem=halo_send.at[f, g],
            recv_sem=halo_recv.at[f, g],
            device_id={"ctx": lax.rem(c + 1, n_ctx)},
            device_id_type=MESH,
        )

    def send_state(g, to, slot):
        return pltpu.make_async_remote_copy(
            src_ref=own_states.at[pl.ds(g * group, group)],
            dst_ref=got_states.at[slot, pl.ds(g * group, group)],
            send_sem=st_send.at[g, to],
            recv_sem=st_recv.at[g, slot],
            device_id={"ctx": to},
            device_id_type=MESH,
        )

    def send_part(g, to, slot):
        return pltpu.make_async_remote_copy(
            src_ref=sbuf.at[to, pl.ds(g * group, group)],
            dst_ref=rbuf.at[slot, pl.ds(g * group, group)],
            send_sem=a_send.at[to, g],
            recv_sem=a_recv.at[slot, g],
            device_id={"tp": to},
            device_id_type=MESH,
        )

    def place(lg, source):
        return out.at[
            pl.ds(lg * group, group), :, pl.ds(pl.multiple_of(source * width, width), width)
        ]

    def forward_remote(buf, layer, g, source):
        return pltpu.make_async_remote_copy(
            src_ref=buf.at[layer, pl.ds(g * group, group)],
            dst_ref=place(lax.rem(g, ngo), source),
            send_sem=b_send.at[layer, g],
            recv_sem=b_recv.at[source, lax.rem(g, ngo)],
            device_id={"ctx": ratio * layer + g // ngo},
            device_id_type=MESH,
        )

    def forward_local(buf, layer, g):
        return pltpu.make_async_copy(
            buf.at[layer, pl.ds(g * group, group)],
            place(lax.rem(g, ngo), c),
            b_recv.at[c, lax.rem(g, ngo)],
        )

    def forward(buf, layer, g):
        target = ratio * layer + g // ngo

        @pl.when(target != c)
        def _():
            forward_remote(buf, layer, g, c).start()

        @pl.when(target == c)
        def _():
            forward_local(buf, layer, g).start()

    barrier = pltpu.get_barrier_semaphore()

    @pl.loop(1, n_ctx)
    def _(d):
        pl.semaphore_signal(
            barrier, inc=1, device_id={"ctx": lax.rem(c + d, n_ctx)}, device_id_type=MESH
        )

    @pl.loop(1, n_tp)
    def _(d):
        pl.semaphore_signal(
            barrier, inc=1, device_id={"tp": lax.rem(z + d, n_tp)}, device_id_type=MESH
        )

    @pl.loop(0, ng)
    def _(g):
        for f in range(3):
            load(f, g).start()

    @pl.when(c == 0)
    def _():
        halo[...] = jnp.zeros_like(halo)

    pl.semaphore_wait(barrier, n_ctx + n_tp - 2)

    @pl.when(c < n_ctx - 1)
    def _():
        @pl.loop(0, ng)
        def _(g):
            for f in range(3):
                send_halo(f, g).start()

    def ready(f, g):
        load(f, g).wait()

        @pl.when(c > 0)
        def _():
            send_halo(f, g).wait_recv()

    def short(f, coef, first, rows, count):
        x = bufs[f][pl.ds(rows, count), :].astype(F32)
        before = halo[f, pl.ds(rows, count), :].astype(F32)
        whole = jnp.concatenate([before, x], axis=1)
        one = pltpu.roll(whole, 1, 1)[:, LANES:]
        two = pltpu.roll(whole, 2, 1)[:, LANES:]
        return coef[:, first : first + 1] * x + (
            coef[:, first + 1 : first + 2] * one + coef[:, first + 2 : first + 3] * two
        )

    def coefficients(h):
        return cols[:, pl.ds(pl.multiple_of(h * hd, hd), hd)].T

    lane = lax.broadcasted_iota(jnp.int32, (1, chunk), 1).astype(F32)
    spot = lax.broadcasted_iota(jnp.int32, (chunk, 1), 0).astype(F32)
    middle = (chunk - 1.0) * 0.5
    nt = (((1,), (1,)), ((), ()))

    def head_states(h):
        coef = coefficients(h)
        base = pl.multiple_of(h * hd, hd)
        for r in range(0, hd, part):
            some = coef[r : r + part]
            rows = pl.multiple_of(base + r, part)
            p = short(0, some, 3, rows, part) * short(1, some, 6, rows, part)
            high = p.astype(BF16)
            phi[pl.ds(rows, part), :] = high
            plo[pl.ds(rows, part), :] = (p - high.astype(F32)).astype(BF16)
        rate = rate_col[h]
        high, low = split2(jnp.exp(-rate * (chunk - 1.0 - lane)))
        both = jnp.concatenate([high, low], axis=0).astype(BF16)
        p_high = jnp.concatenate(
            [phi[pl.ds(base, hd), j * chunk : (j + 1) * chunk] for j in range(nch)], axis=0
        )
        p_low = jnp.concatenate(
            [plo[pl.ds(base, hd), j * chunk : (j + 1) * chunk] for j in range(nch)], axis=0
        )
        first = lax.dot_general(both, p_high, nt, preferred_element_type=F32)
        second = lax.dot_general(high.astype(BF16), p_low, nt, preferred_element_type=F32)
        total = first[:modes] + (first[modes:] + second)
        chunk_states[h] = total
        step = jnp.exp(-rate * float(chunk))
        state = total[:, :hd]
        for j in range(1, nch):
            state = step * state + total[:, j * hd : (j + 1) * hd]
        own_states[h] = state

    def group_states(g):
        ready(0, g)
        ready(1, g)

        @pl.loop(0, group)
        def _(i):
            head_states(g * group + i)

        @pl.loop(c + 1, n_ctx)
        def _(to):
            send_state(g, to, c).start()

    def head_gated(h):
        coef = coefficients(h)
        base = pl.multiple_of(h * hd, hd)
        rate, weight = rate_col[h], weight_col[h]
        rising = jnp.exp(rate_row[h] * (spot - middle))
        falling = weight * jnp.exp(-rate * (lane - middle))
        full = lax.dot_general(
            rising, falling, (((1,), (0,)), ((), ())),
            precision=lax.Precision.HIGHEST, preferred_element_type=F32,
        )
        causal = lax.broadcasted_iota(jnp.int32, (chunk, chunk), 1) >= lax.broadcasted_iota(
            jnp.int32, (chunk, chunk), 0
        )
        t_high, t_low = split2(jnp.where(causal, full, 0.0))
        t_high, t_low = t_high.astype(BF16), t_low.astype(BF16)
        whole = jnp.exp(-rate * float(width))
        state = lax.fori_loop(
            0, c, lambda k, s: whole * s + got_states[k, h], jnp.zeros((modes, hd), F32)
        )
        step = jnp.exp(-rate * float(chunk))
        mine = chunk_states[h]
        states = [state]
        for j in range(nch - 1):
            states.append(step * states[-1] + mine[:, j * hd : (j + 1) * hd])
        e_high, e_low = split2(jnp.concatenate(states, axis=1))
        e_all = jnp.concatenate([e_high, e_low, e_high], axis=0).T.astype(BF16)
        f_high, f_low = split2(weight * jnp.exp(-rate * (lane + 1.0)))
        f_all = jnp.concatenate([f_high, f_high, f_low], axis=0).astype(BF16)
        p_high = jnp.concatenate(
            [phi[pl.ds(base, hd), j * chunk : (j + 1) * chunk] for j in range(nch)], axis=0
        )
        p_low = jnp.concatenate(
            [plo[pl.ds(base, hd), j * chunk : (j + 1) * chunk] for j in range(nch)], axis=0
        )
        acc[...] = (
            jnp.dot(p_high, t_high, preferred_element_type=F32)
            + jnp.dot(p_low, t_high, preferred_element_type=F32)
            + jnp.dot(p_high, t_low, preferred_element_type=F32)
            + jnp.dot(e_all, f_all, preferred_element_type=F32)
        )
        for r in range(n_tp):
            some = coef[r * part : (r + 1) * part]
            rows = pl.multiple_of(base + r * part, part)
            gate = short(2, some, 0, rows, part)
            p = phi[pl.ds(rows, part), :].astype(F32) + plo[pl.ds(rows, part), :].astype(F32)
            conv = jnp.concatenate(
                [acc[j * hd + r * part : j * hd + (r + 1) * part, :] for j in range(nch)], axis=1
            )
            sbuf[r, h] = (gate * (conv + some[:, 9:10] * p)).astype(BF16)

    def group_gated(g):
        @pl.loop(0, c)
        def _(k):
            send_state(g, c, k).wait_recv()

        ready(2, g)

        @pl.loop(0, group)
        def _(i):
            head_gated(g * group + i)

        @pl.loop(1, n_tp)
        def _(d):
            send_part(g, lax.rem(z + d, n_tp), z).start()

        forward(sbuf, z, g)

    ahead = min(2, ng)
    for g in range(ahead):
        group_states(g)

    @pl.loop(0, ng)
    def _(g):
        group_gated(g)

        @pl.when(g + ahead < ng)
        def _():
            group_states(g + ahead)

    @pl.loop(0, ng)
    def _(g):
        @pl.loop(1, n_tp)
        def _(d):
            layer = lax.rem(z + d, n_tp)
            send_part(g, z, layer).wait_recv()
            forward(rbuf, layer, g)

    @pl.loop(0, ng)
    def _(g):
        @pl.when(c < n_ctx - 1)
        def _():
            for f in range(3):
                send_halo(f, g).wait_send()

        @pl.loop(c + 1, n_ctx)
        def _(to):
            send_state(g, to, c).wait_send()

        @pl.loop(1, n_tp)
        def _(d):
            send_part(g, lax.rem(z + d, n_tp), z).wait_send()

        @pl.loop(0, n_tp)
        def _(layer):
            @pl.when(ratio * layer + g // ngo != c)
            def _():
                forward_remote(rbuf, layer, g, c).wait_send()

    mine = c // ratio
    hout = lax.rem(c, ratio)

    @pl.loop(0, ngo)
    def _(lg):
        g = hout * ngo + lg

        @pl.loop(0, n_ctx)
        def _(source):
            @pl.when(source != c)
            def _():
                forward_remote(rbuf, mine, g, source).wait_recv()

            @pl.when(source == c)
            def _():
                forward_local(rbuf, mine, g).wait()


def per_device(n_ctx, n_tp, query_feat, key_feat, value_feat, short_filter, skip, decay_rate, residue):
    channels, width = query_feat.shape
    heads, modes = decay_rate.shape
    hd = channels // heads
    heads_out = heads * n_tp // n_ctx
    group = 2 if heads_out % 2 == 0 else 1
    chunk = min(256, width)
    ng = heads // group
    ngo = heads_out // group
    part = hd // n_tp
    size = (n_ctx, n_tp, heads, hd, width, modes, chunk, group)
    cols = jnp.concatenate(
        [short_filter.reshape(9, channels), skip[None], jnp.zeros((6, channels), F32)], axis=0
    )
    vmem = pl.BlockSpec(memory_space=pltpu.VMEM)
    hbm = pl.BlockSpec(memory_space=pl.ANY)
    dma = pltpu.SemaphoreType.DMA
    return pl.pallas_call(
        functools.partial(kernel, size),
        out_shape=jax.ShapeDtypeStruct((heads_out, part, width * n_ctx), BF16),
        in_specs=[hbm, hbm, hbm, vmem, vmem, vmem, vmem],
        out_specs=hbm,
        scratch_shapes=[
            pltpu.VMEM((channels, width), BF16),
            pltpu.VMEM((channels, width), BF16),
            pltpu.VMEM((channels, width), BF16),
            pltpu.VMEM((3, channels, LANES), BF16),
            pltpu.VMEM((channels, width), BF16),
            pltpu.VMEM((channels, width), BF16),
            pltpu.VMEM((hd * width // chunk, chunk), F32),
            pltpu.VMEM((n_tp, heads, part, width), BF16),
            pltpu.VMEM((n_tp, heads, part, width), BF16),
            pltpu.VMEM((heads, modes, hd * width // chunk), F32),
            pltpu.VMEM((heads, modes, hd), F32),
            pltpu.VMEM((n_ctx, heads, modes, hd), F32),
            dma((3, ng)),
            dma((3, ng)),
            dma((3, ng)),
            dma((ng, n_ctx)),
            dma((ng, n_ctx)),
            dma((n_tp, ng)),
            dma((n_tp, ng)),
            dma((n_tp, ng)),
            dma((n_ctx, ngo)),
        ],
        compiler_params=pltpu.CompilerParams(
            collective_id=0, has_side_effects=True, vmem_limit_bytes=50 * 1024 * 1024
        ),
        cost_estimate=pl.CostEstimate(
            flops=2 * channels * width * 1024, bytes_accessed=8 * channels * width, transcendentals=0
        ),
    )(
        query_feat, key_feat, value_feat, cols,
        decay_rate[:, None, :], decay_rate[:, :, None], residue[:, :, None],
    )


def solution(mesh):
    return jax.shard_map(
        functools.partial(per_device, mesh.shape["ctx"], mesh.shape["tp"]),
        mesh=mesh,
        in_specs=(
            P("tp", "ctx"),
            P("tp", "ctx"),
            P("tp", "ctx"),
            P(None, None, "tp"),
            P("tp"),
            P("tp", None),
            P("tp", None),
        ),
        out_specs=P("ctx", "tp", None),
        check_vma=False,
    )
```

```python
import functools

import jax
import jax.numpy as jnp
from jax import lax
from jax.experimental import pallas as pl
from jax.experimental.pallas import tpu as pltpu
from jax.sharding import PartitionSpec as P

LANES = 128
MESH = pl.DeviceIdType.MESH
F32 = jnp.float32
BF16 = jnp.bfloat16


def split2(x):
    high = x.astype(BF16).astype(F32)
    return high, x - high


def kernel(
    size, q_hbm, k_hbm, v_hbm, filters, skip, decay, residue, out,
    qbuf, kbuf, vbuf, cols, edge, last, halo, phi, plo, acc, sbuf, rbuf, chunk_states, own_states, got_states,
    in_sem, edge_sem, halo_send, halo_recv, st_send, st_recv, a_send, a_recv, b_send, b_recv,
):
    n_ctx, n_tp, heads, hd, width, modes, chunk, group = size
    c = lax.axis_index("ctx")
    z = lax.axis_index("tp")
    ng = heads // group
    rows_g = group * hd
    ratio = n_ctx // n_tp
    heads_out = heads // ratio
    ngo = heads_out // group
    part = hd // n_tp
    nch = width // chunk
    hbms = (k_hbm, v_hbm, q_hbm)
    bufs = (kbuf, vbuf, qbuf)

    def load(f, g):
        rows = pl.ds(pl.multiple_of(g * rows_g, rows_g), rows_g)
        return pltpu.make_async_copy(hbms[f].at[rows], bufs[f].at[rows], in_sem.at[f, g])

    def load_edge(f):
        return pltpu.make_async_copy(
            hbms[f].at[:, pl.ds(width - LANES, LANES)], edge.at[f], edge_sem.at[f]
        )

    def send_halo():
        return pltpu.make_async_remote_copy(
            src_ref=last,
            dst_ref=halo,
            send_sem=halo_send,
            recv_sem=halo_recv,
            device_id={"ctx": lax.rem(c + 1, n_ctx)},
            device_id_type=MESH,
        )

    def send_state(g, to, slot):
        return pltpu.make_async_remote_copy(
            src_ref=own_states.at[pl.ds(g * group, group)],
            dst_ref=got_states.at[slot, pl.ds(g * group, group)],
            send_sem=st_send.at[g, to],
            recv_sem=st_recv.at[g, slot],
            device_id={"ctx": to},
            device_id_type=MESH,
        )

    def send_part(g, to, slot):
        return pltpu.make_async_remote_copy(
            src_ref=sbuf.at[to, pl.ds(g * group, group)],
            dst_ref=rbuf.at[slot, pl.ds(g * group, group)],
            send_sem=a_send.at[to, g],
            recv_sem=a_recv.at[slot, g],
            device_id={"tp": to},
            device_id_type=MESH,
        )

    def place(lg, source):
        return out.at[
            pl.ds(lg * group, group), :, pl.ds(pl.multiple_of(source * width, width), width)
        ]

    def forward_remote(buf, layer, g, source):
        return pltpu.make_async_remote_copy(
            src_ref=buf.at[layer, pl.ds(g * group, group)],
            dst_ref=place(lax.rem(g, ngo), source),
            send_sem=b_send.at[layer, g],
            recv_sem=b_recv.at[source, lax.rem(g, ngo)],
            device_id={"ctx": ratio * layer + g // ngo},
            device_id_type=MESH,
        )

    def forward_local(buf, layer, g):
        return pltpu.make_async_copy(
            buf.at[layer, pl.ds(g * group, group)],
            place(lax.rem(g, ngo), c),
            b_recv.at[c, lax.rem(g, ngo)],
        )

    def forward(buf, layer, g):
        target = ratio * layer + g // ngo

        @pl.when(target != c)
        def _():
            forward_remote(buf, layer, g, c).start()

        @pl.when(target == c)
        def _():
            forward_local(buf, layer, g).start()

    barrier = pltpu.get_barrier_semaphore()

    @pl.loop(1, n_ctx)
    def _(d):
        pl.semaphore_signal(
            barrier, inc=1, device_id={"ctx": lax.rem(c + d, n_ctx)}, device_id_type=MESH
        )

    @pl.loop(1, n_tp)
    def _(d):
        pl.semaphore_signal(
            barrier, inc=1, device_id={"tp": lax.rem(z + d, n_tp)}, device_id_type=MESH
        )

    for f in range(3):
        load_edge(f).start()

    @pl.loop(0, ng)
    def _(g):
        for f in range(3):
            load(f, g).start()

    cols[...] = jnp.zeros_like(cols)
    for f in range(3):
        cols[3 * f : 3 * f + 3, :] = filters[f]
    cols[9:10, :] = skip[...]

    @pl.when(c == 0)
    def _():
        halo[...] = jnp.zeros_like(halo)

    row = lax.broadcasted_iota(jnp.int32, (8, LANES), 0)
    token = lax.broadcasted_iota(jnp.int32, (8, LANES), 1)
    for f in range(3):
        load_edge(f).wait()

    @pl.loop(0, heads)
    def _(h):
        at = pl.ds(pl.multiple_of(h * hd, hd), hd)
        picked = jnp.zeros((8, hd), F32)
        for f in range(3):
            pick = jnp.where((row >> 1 == f) & (token == LANES - 2 + (row & 1)), 1.0, 0.0)
            picked = picked + lax.dot_general(
                pick.astype(BF16), edge[f, at, :], (((1,), (1,)), ((), ())),
                preferred_element_type=F32,
            )
        last[:, at] = picked

    pl.semaphore_wait(barrier, n_ctx + n_tp - 2)

    @pl.when(c < n_ctx - 1)
    def _():
        send_halo().start()

    @pl.when(c > 0)
    def _():
        send_halo().wait_recv()

    final = lax.broadcasted_iota(jnp.int32, (part, LANES), 1) == LANES - 1

    def short(f, coef, first, rows, count):
        x = bufs[f][pl.ds(rows, count), :].astype(F32)
        before = jnp.where(final, coef[:, 17 + 2 * f : 18 + 2 * f], coef[:, 16 + 2 * f : 17 + 2 * f])
        whole = jnp.concatenate([before, x], axis=1)
        one = pltpu.roll(whole, 1, 1)[:, LANES:]
        two = pltpu.roll(whole, 2, 1)[:, LANES:]
        return coef[:, first : first + 1] * x + (
            coef[:, first + 1 : first + 2] * one + coef[:, first + 2 : first + 3] * two
        )

    def coefficients(h):
        at = pl.ds(pl.multiple_of(h * hd, hd), hd)
        return jnp.concatenate([cols[:, at], halo[:, at]], axis=0).T

    diagonal = lax.broadcasted_iota(jnp.int32, (modes, modes), 0) == lax.broadcasted_iota(
        jnp.int32, (modes, modes), 1
    )

    def column(ref, h):
        return jnp.sum(jnp.where(diagonal, ref[pl.ds(h, 1), :], 0.0), axis=1, keepdims=True)

    lane = lax.broadcasted_iota(jnp.int32, (1, chunk), 1).astype(F32)
    spot = lax.broadcasted_iota(jnp.int32, (chunk, 1), 0).astype(F32)
    middle = (chunk - 1.0) * 0.5
    nt = (((1,), (1,)), ((), ()))

    def head_states(h):
        coef = coefficients(h)
        base = pl.multiple_of(h * hd, hd)
        for r in range(0, hd, part):
            some = coef[r : r + part]
            rows = pl.multiple_of(base + r, part)
            p = short(0, some, 3, rows, part) * short(1, some, 6, rows, part)
            high = p.astype(BF16)
            phi[pl.ds(rows, part), :] = high
            plo[pl.ds(rows, part), :] = (p - high.astype(F32)).astype(BF16)
        rate = column(decay, h)
        high, low = split2(jnp.exp(-rate * (chunk - 1.0 - lane)))
        both = jnp.concatenate([high, low], axis=0).astype(BF16)
        p_high = jnp.concatenate(
            [phi[pl.ds(base, hd), j * chunk : (j + 1) * chunk] for j in range(nch)], axis=0
        )
        p_low = jnp.concatenate(
            [plo[pl.ds(base, hd), j * chunk : (j + 1) * chunk] for j in range(nch)], axis=0
        )
        first = lax.dot_general(both, p_high, nt, preferred_element_type=F32)
        second = lax.dot_general(high.astype(BF16), p_low, nt, preferred_element_type=F32)
        total = first[:modes] + (first[modes:] + second)
        chunk_states[h] = total
        step = jnp.exp(-rate * float(chunk))
        state = total[:, :hd]
        for j in range(1, nch):
            state = step * state + total[:, j * hd : (j + 1) * hd]
        own_states[h] = state

    def group_states(g):
        load(0, g).wait()
        load(1, g).wait()

        @pl.loop(0, group)
        def _(i):
            head_states(g * group + i)

        @pl.loop(c + 1, n_ctx)
        def _(to):
            send_state(g, to, c).start()

    def head_gated(h):
        coef = coefficients(h)
        base = pl.multiple_of(h * hd, hd)
        rate, weight = column(decay, h), column(residue, h)
        rising = jnp.exp(decay[pl.ds(h, 1), :] * (spot - middle))
        falling = weight * jnp.exp(-rate * (lane - middle))
        full = lax.dot_general(
            rising, falling, (((1,), (0,)), ((), ())),
            precision=lax.Precision.HIGHEST, preferred_element_type=F32,
        )
        causal = lax.broadcasted_iota(jnp.int32, (chunk, chunk), 1) >= lax.broadcasted_iota(
            jnp.int32, (chunk, chunk), 0
        )
        t_high, t_low = split2(jnp.where(causal, full, 0.0))
        t_high, t_low = t_high.astype(BF16), t_low.astype(BF16)
        whole = jnp.exp(-rate * float(width))
        state = lax.fori_loop(
            0, c, lambda k, s: whole * s + got_states[k, h], jnp.zeros((modes, hd), F32)
        )
        step = jnp.exp(-rate * float(chunk))
        mine = chunk_states[h]
        states = [state]
        for j in range(nch - 1):
            states.append(step * states[-1] + mine[:, j * hd : (j + 1) * hd])
        e_high, e_low = split2(jnp.concatenate(states, axis=1))
        e_all = jnp.concatenate([e_high, e_low, e_high], axis=0).T.astype(BF16)
        f_high, f_low = split2(weight * jnp.exp(-rate * (lane + 1.0)))
        f_all = jnp.concatenate([f_high, f_high, f_low], axis=0).astype(BF16)
        p_high = jnp.concatenate(
            [phi[pl.ds(base, hd), j * chunk : (j + 1) * chunk] for j in range(nch)], axis=0
        )
        p_low = jnp.concatenate(
            [plo[pl.ds(base, hd), j * chunk : (j + 1) * chunk] for j in range(nch)], axis=0
        )
        acc[...] = (
            jnp.dot(p_high, t_high, preferred_element_type=F32)
            + jnp.dot(p_low, t_high, preferred_element_type=F32)
            + jnp.dot(p_high, t_low, preferred_element_type=F32)
            + jnp.dot(e_all, f_all, preferred_element_type=F32)
        )
        for r in range(n_tp):
            some = coef[r * part : (r + 1) * part]
            rows = pl.multiple_of(base + r * part, part)
            gate = short(2, some, 0, rows, part)
            p = phi[pl.ds(rows, part), :].astype(F32) + plo[pl.ds(rows, part), :].astype(F32)
            conv = jnp.concatenate(
                [acc[j * hd + r * part : j * hd + (r + 1) * part, :] for j in range(nch)], axis=1
            )
            sbuf[r, h] = (gate * (conv + some[:, 9:10] * p)).astype(BF16)

    def group_gated(g):
        @pl.loop(0, c)
        def _(k):
            send_state(g, c, k).wait_recv()

        load(2, g).wait()

        @pl.loop(0, group)
        def _(i):
            head_gated(g * group + i)

        @pl.loop(1, n_tp)
        def _(d):
            send_part(g, lax.rem(z + d, n_tp), z).start()


    ahead = min(2, ng)
    for g in range(ahead):
        group_states(g)

    @pl.loop(0, ng)
    def _(g):
        group_gated(g)

        @pl.when(g + ahead < ng)
        def _():
            group_states(g + ahead)

    @pl.loop(0, ng)
    def _(g):
        @pl.loop(0, n_tp)
        def _(d):
            layer = lax.rem(c // ratio + d, n_tp)

            @pl.when(layer == z)
            def _():
                forward(sbuf, layer, g)

            @pl.when(layer != z)
            def _():
                send_part(g, z, layer).wait_recv()
                forward(rbuf, layer, g)

    @pl.when(c < n_ctx - 1)
    def _():
        send_halo().wait_send()

    @pl.loop(0, ng)
    def _(g):
        @pl.loop(c + 1, n_ctx)
        def _(to):
            send_state(g, to, c).wait_send()

        @pl.loop(1, n_tp)
        def _(d):
            send_part(g, lax.rem(z + d, n_tp), z).wait_send()

        @pl.loop(0, n_tp)
        def _(layer):
            @pl.when(ratio * layer + g // ngo != c)
            def _():
                forward_remote(rbuf, layer, g, c).wait_send()

    mine = c // ratio
    hout = lax.rem(c, ratio)

    @pl.loop(0, ngo)
    def _(lg):
        g = hout * ngo + lg

        @pl.loop(0, n_ctx)
        def _(source):
            @pl.when(source != c)
            def _():
                forward_remote(rbuf, mine, g, source).wait_recv()

            @pl.when(source == c)
            def _():
                forward_local(rbuf, mine, g).wait()


def per_device(n_ctx, n_tp, query_feat, key_feat, value_feat, short_filter, skip, decay_rate, residue):
    channels, width = query_feat.shape
    heads, modes = decay_rate.shape
    hd = channels // heads
    heads_out = heads * n_tp // n_ctx
    group = 2 if heads_out % 2 == 0 else 1
    chunk = min(256, width)
    ng = heads // group
    ngo = heads_out // group
    part = hd // n_tp
    size = (n_ctx, n_tp, heads, hd, width, modes, chunk, group)
    vmem = pl.BlockSpec(memory_space=pltpu.VMEM)
    hbm = pl.BlockSpec(memory_space=pl.ANY)
    dma = pltpu.SemaphoreType.DMA
    return pl.pallas_call(
        functools.partial(kernel, size),
        out_shape=jax.ShapeDtypeStruct((heads_out, part, width * n_ctx), BF16),
        in_specs=[hbm, hbm, hbm, vmem, vmem, vmem, vmem],
        out_specs=hbm,
        scratch_shapes=[
            pltpu.VMEM((channels, width), BF16),
            pltpu.VMEM((channels, width), BF16),
            pltpu.VMEM((channels, width), BF16),
            pltpu.VMEM((16, channels), F32),
            pltpu.VMEM((3, channels, LANES), BF16),
            pltpu.VMEM((8, channels), F32),
            pltpu.VMEM((8, channels), F32),
            pltpu.VMEM((channels, width), BF16),
            pltpu.VMEM((channels, width), BF16),
            pltpu.VMEM((hd * width // chunk, chunk), F32),
            pltpu.VMEM((n_tp, heads, part, width), BF16),
            pltpu.VMEM((n_tp, heads, part, width), BF16),
            pltpu.VMEM((heads, modes, hd * width // chunk), F32),
            pltpu.VMEM((heads, modes, hd), F32),
            pltpu.VMEM((n_ctx, heads, modes, hd), F32),
            dma((3, ng)),
            dma((3,)),
            dma(()),
            dma(()),
            dma((ng, n_ctx)),
            dma((ng, n_ctx)),
            dma((n_tp, ng)),
            dma((n_tp, ng)),
            dma((n_tp, ng)),
            dma((n_ctx, ngo)),
        ],
        compiler_params=pltpu.CompilerParams(
            collective_id=0, has_side_effects=True, vmem_limit_bytes=50 * 1024 * 1024
        ),
        cost_estimate=pl.CostEstimate(
            flops=2 * channels * width * 1024, bytes_accessed=8 * channels * width, transcendentals=0
        ),
    )(
        query_feat, key_feat, value_feat, short_filter, skip[None], decay_rate, residue
    )


def solution(mesh):
    return jax.shard_map(
        functools.partial(per_device, mesh.shape["ctx"], mesh.shape["tp"]),
        mesh=mesh,
        in_specs=(
            P("tp", "ctx"),
            P("tp", "ctx"),
            P("tp", "ctx"),
            P(None, None, "tp"),
            P("tp"),
            P("tp", None),
            P("tp", None),
        ),
        out_specs=P("ctx", "tp", None),
        check_vma=False,
    )
```

```python
import functools

import jax
import jax.numpy as jnp
from jax import lax
from jax.experimental import pallas as pl
from jax.experimental.pallas import tpu as pltpu
from jax.sharding import PartitionSpec as P

LANES = 128
MESH = pl.DeviceIdType.MESH
F32 = jnp.float32
BF16 = jnp.bfloat16


def split2(x):
    high = x.astype(BF16).astype(F32)
    return high, x - high


def kernel(
    size, q_hbm, k_hbm, v_hbm, filters, skip, decay, residue, out,
    qbuf, kbuf, vbuf, cols, edge, last, halo, phi, plo, acc, sbuf, rbuf, chunk_states, own_states, got_states,
    in_sem, edge_sem, halo_send, halo_recv, st_send, st_recv, a_send, a_recv, b_send, b_recv,
):
    n_ctx, n_tp, heads, hd, width, modes, chunk, group = size
    c = lax.axis_index("ctx")
    z = lax.axis_index("tp")
    ng = heads // group
    rows_g = group * hd
    ratio = n_ctx // n_tp
    heads_out = heads // ratio
    ngo = heads_out // group
    part = hd // n_tp
    nch = width // chunk
    hbms = (k_hbm, v_hbm, q_hbm)
    bufs = (kbuf, vbuf, qbuf)

    def load(f, g):
        rows = pl.ds(pl.multiple_of(g * rows_g, rows_g), rows_g)
        return pltpu.make_async_copy(hbms[f].at[rows], bufs[f].at[rows], in_sem.at[f, g])

    def load_edge(f):
        return pltpu.make_async_copy(
            hbms[f].at[:, pl.ds(width - LANES, LANES)], edge.at[f], edge_sem.at[f]
        )

    def send_halo():
        return pltpu.make_async_remote_copy(
            src_ref=last,
            dst_ref=halo,
            send_sem=halo_send,
            recv_sem=halo_recv,
            device_id={"ctx": lax.rem(c + 1, n_ctx)},
            device_id_type=MESH,
        )

    def send_state(g, to, slot):
        return pltpu.make_async_remote_copy(
            src_ref=own_states.at[pl.ds(g * group, group)],
            dst_ref=got_states.at[slot, pl.ds(g * group, group)],
            send_sem=st_send.at[g, to],
            recv_sem=st_recv.at[g, slot],
            device_id={"ctx": to},
            device_id_type=MESH,
        )

    def send_part(g, to, slot):
        return pltpu.make_async_remote_copy(
            src_ref=sbuf.at[to, pl.ds(g * group, group)],
            dst_ref=rbuf.at[slot, pl.ds(g * group, group)],
            send_sem=a_send.at[to, g],
            recv_sem=a_recv.at[slot, g],
            device_id={"tp": to},
            device_id_type=MESH,
        )

    def send_head(g, i, to, slot):
        return pltpu.make_async_remote_copy(
            src_ref=sbuf.at[to, pl.ds(g * group + i, 1)],
            dst_ref=rbuf.at[slot, pl.ds(g * group + i, 1)],
            send_sem=a_send.at[to, g],
            recv_sem=a_recv.at[slot, g],
            device_id={"tp": to},
            device_id_type=MESH,
        )

    def place(lg, source):
        return out.at[
            pl.ds(lg * group, group), :, pl.ds(pl.multiple_of(source * width, width), width)
        ]

    def forward_remote(buf, layer, g, source):
        return pltpu.make_async_remote_copy(
            src_ref=buf.at[layer, pl.ds(g * group, group)],
            dst_ref=place(lax.rem(g, ngo), source),
            send_sem=b_send.at[layer, g],
            recv_sem=b_recv.at[source, lax.rem(g, ngo)],
            device_id={"ctx": ratio * layer + g // ngo},
            device_id_type=MESH,
        )

    def forward_local(buf, layer, g):
        return pltpu.make_async_copy(
            buf.at[layer, pl.ds(g * group, group)],
            place(lax.rem(g, ngo), c),
            b_recv.at[c, lax.rem(g, ngo)],
        )

    def forward(buf, layer, g):
        target = ratio * layer + g // ngo

        @pl.when(target != c)
        def _():
            forward_remote(buf, layer, g, c).start()

        @pl.when(target == c)
        def _():
            forward_local(buf, layer, g).start()

    barrier = pltpu.get_barrier_semaphore()

    @pl.loop(1, n_ctx)
    def _(d):
        pl.semaphore_signal(
            barrier, inc=1, device_id={"ctx": lax.rem(c + d, n_ctx)}, device_id_type=MESH
        )

    @pl.loop(1, n_tp)
    def _(d):
        pl.semaphore_signal(
            barrier, inc=1, device_id={"tp": lax.rem(z + d, n_tp)}, device_id_type=MESH
        )

    for f in range(3):
        load_edge(f).start()

    @pl.loop(0, ng)
    def _(g):
        for f in range(3):
            load(f, g).start()

    cols[...] = jnp.zeros_like(cols)
    for f in range(3):
        cols[3 * f : 3 * f + 3, :] = filters[f]
    cols[9:10, :] = skip[...]

    @pl.when(c == 0)
    def _():
        halo[...] = jnp.zeros_like(halo)

    row = lax.broadcasted_iota(jnp.int32, (8, LANES), 0)
    token = lax.broadcasted_iota(jnp.int32, (8, LANES), 1)
    for f in range(3):
        load_edge(f).wait()

    @pl.loop(0, heads)
    def _(h):
        at = pl.ds(pl.multiple_of(h * hd, hd), hd)
        picked = jnp.zeros((8, hd), F32)
        for f in range(3):
            pick = jnp.where((row >> 1 == f) & (token == LANES - 2 + (row & 1)), 1.0, 0.0)
            picked = picked + lax.dot_general(
                pick.astype(BF16), edge[f, at, :], (((1,), (1,)), ((), ())),
                preferred_element_type=F32,
            )
        last[:, at] = picked

    pl.semaphore_wait(barrier, n_ctx + n_tp - 2)

    @pl.when(c < n_ctx - 1)
    def _():
        send_halo().start()

    @pl.when(c > 0)
    def _():
        send_halo().wait_recv()

    final = lax.broadcasted_iota(jnp.int32, (part, LANES), 1) == LANES - 1

    def short(f, coef, first, rows, count):
        x = bufs[f][pl.ds(rows, count), :].astype(F32)
        before = jnp.where(final, coef[:, 17 + 2 * f : 18 + 2 * f], coef[:, 16 + 2 * f : 17 + 2 * f])
        whole = jnp.concatenate([before, x], axis=1)
        one = pltpu.roll(whole, 1, 1)[:, LANES:]
        two = pltpu.roll(whole, 2, 1)[:, LANES:]
        return coef[:, first : first + 1] * x + (
            coef[:, first + 1 : first + 2] * one + coef[:, first + 2 : first + 3] * two
        )

    def coefficients(h):
        at = pl.ds(pl.multiple_of(h * hd, hd), hd)
        return jnp.concatenate([cols[:, at], halo[:, at]], axis=0).T

    diagonal = lax.broadcasted_iota(jnp.int32, (modes, modes), 0) == lax.broadcasted_iota(
        jnp.int32, (modes, modes), 1
    )

    def column(ref, h):
        return jnp.sum(jnp.where(diagonal, ref[pl.ds(h, 1), :], 0.0), axis=1, keepdims=True)

    lane = lax.broadcasted_iota(jnp.int32, (1, chunk), 1).astype(F32)
    spot = lax.broadcasted_iota(jnp.int32, (chunk, 1), 0).astype(F32)
    middle = (chunk - 1.0) * 0.5
    nt = (((1,), (1,)), ((), ()))

    def head_states(h):
        coef = coefficients(h)
        base = pl.multiple_of(h * hd, hd)
        for r in range(0, hd, part):
            some = coef[r : r + part]
            rows = pl.multiple_of(base + r, part)
            p = short(0, some, 3, rows, part) * short(1, some, 6, rows, part)
            high = p.astype(BF16)
            phi[pl.ds(rows, part), :] = high
            plo[pl.ds(rows, part), :] = (p - high.astype(F32)).astype(BF16)
        rate = column(decay, h)
        high, low = split2(jnp.exp(-rate * (chunk - 1.0 - lane)))
        both = jnp.concatenate([high, low], axis=0).astype(BF16)
        p_high = jnp.concatenate(
            [phi[pl.ds(base, hd), j * chunk : (j + 1) * chunk] for j in range(nch)], axis=0
        )
        p_low = jnp.concatenate(
            [plo[pl.ds(base, hd), j * chunk : (j + 1) * chunk] for j in range(nch)], axis=0
        )
        first = lax.dot_general(both, p_high, nt, preferred_element_type=F32)
        second = lax.dot_general(high.astype(BF16), p_low, nt, preferred_element_type=F32)
        total = first[:modes] + (first[modes:] + second)
        chunk_states[h] = total
        step = jnp.exp(-rate * float(chunk))
        state = total[:, :hd]
        for j in range(1, nch):
            state = step * state + total[:, j * hd : (j + 1) * hd]
        own_states[h] = state

    def group_states(g):
        load(0, g).wait()
        load(1, g).wait()

        @pl.loop(0, group)
        def _(i):
            head_states(g * group + i)

        @pl.loop(c + 1, n_ctx)
        def _(to):
            send_state(g, to, c).start()

    def head_gated(h):
        coef = coefficients(h)
        base = pl.multiple_of(h * hd, hd)
        rate, weight = column(decay, h), column(residue, h)
        rising = jnp.exp(decay[pl.ds(h, 1), :] * (spot - middle))
        falling = weight * jnp.exp(-rate * (lane - middle))
        full = lax.dot_general(
            rising, falling, (((1,), (0,)), ((), ())),
            precision=lax.Precision.HIGHEST, preferred_element_type=F32,
        )
        causal = lax.broadcasted_iota(jnp.int32, (chunk, chunk), 1) >= lax.broadcasted_iota(
            jnp.int32, (chunk, chunk), 0
        )
        t_high, t_low = split2(jnp.where(causal, full, 0.0))
        t_high, t_low = t_high.astype(BF16), t_low.astype(BF16)
        whole = jnp.exp(-rate * float(width))
        state = lax.fori_loop(
            0, c, lambda k, s: whole * s + got_states[k, h], jnp.zeros((modes, hd), F32)
        )
        step = jnp.exp(-rate * float(chunk))
        mine = chunk_states[h]
        states = [state]
        for j in range(nch - 1):
            states.append(step * states[-1] + mine[:, j * hd : (j + 1) * hd])
        e_high, e_low = split2(jnp.concatenate(states, axis=1))
        e_all = jnp.concatenate([e_high, e_low, e_high], axis=0).T.astype(BF16)
        f_high, f_low = split2(weight * jnp.exp(-rate * (lane + 1.0)))
        f_all = jnp.concatenate([f_high, f_high, f_low], axis=0).astype(BF16)
        p_high = jnp.concatenate(
            [phi[pl.ds(base, hd), j * chunk : (j + 1) * chunk] for j in range(nch)], axis=0
        )
        p_low = jnp.concatenate(
            [plo[pl.ds(base, hd), j * chunk : (j + 1) * chunk] for j in range(nch)], axis=0
        )
        acc[...] = (
            jnp.dot(p_high, t_high, preferred_element_type=F32)
            + jnp.dot(p_low, t_high, preferred_element_type=F32)
            + jnp.dot(p_high, t_low, preferred_element_type=F32)
            + jnp.dot(e_all, f_all, preferred_element_type=F32)
        )
        for r in range(n_tp):
            some = coef[r * part : (r + 1) * part]
            rows = pl.multiple_of(base + r * part, part)
            gate = short(2, some, 0, rows, part)
            p = phi[pl.ds(rows, part), :].astype(F32) + plo[pl.ds(rows, part), :].astype(F32)
            conv = jnp.concatenate(
                [acc[j * hd + r * part : j * hd + (r + 1) * part, :] for j in range(nch)], axis=1
            )
            sbuf[r, h] = (gate * (conv + some[:, 9:10] * p)).astype(BF16)

    def group_gated(g):
        @pl.loop(0, c)
        def _(k):
            send_state(g, c, k).wait_recv()

        load(2, g).wait()

        @pl.loop(0, group)
        def _(i):
            head_gated(g * group + i)

            @pl.loop(1, n_tp)
            def _(d):
                send_head(g, i, lax.rem(z + d, n_tp), z).start()


    ahead = min(2, ng)
    for g in range(ahead):
        group_states(g)

    @pl.loop(0, ng)
    def _(g):
        group_gated(g)

        @pl.when(g + ahead < ng)
        def _():
            group_states(g + ahead)

    @pl.loop(0, ng)
    def _(g):
        @pl.loop(0, n_tp)
        def _(d):
            layer = lax.rem(c // ratio + d, n_tp)

            @pl.when(layer == z)
            def _():
                forward(sbuf, layer, g)

            @pl.when(layer != z)
            def _():
                send_part(g, z, layer).wait_recv()
                forward(rbuf, layer, g)

    @pl.when(c < n_ctx - 1)
    def _():
        send_halo().wait_send()

    @pl.loop(0, ng)
    def _(g):
        @pl.loop(c + 1, n_ctx)
        def _(to):
            send_state(g, to, c).wait_send()

        @pl.loop(1, n_tp)
        def _(d):
            send_part(g, lax.rem(z + d, n_tp), z).wait_send()

        @pl.loop(0, n_tp)
        def _(layer):
            @pl.when(ratio * layer + g // ngo != c)
            def _():
                forward_remote(rbuf, layer, g, c).wait_send()

    mine = c // ratio
    hout = lax.rem(c, ratio)

    @pl.loop(0, ngo)
    def _(lg):
        g = hout * ngo + lg

        @pl.loop(0, n_ctx)
        def _(source):
            @pl.when(source != c)
            def _():
                forward_remote(rbuf, mine, g, source).wait_recv()

            @pl.when(source == c)
            def _():
                forward_local(rbuf, mine, g).wait()


def per_device(n_ctx, n_tp, query_feat, key_feat, value_feat, short_filter, skip, decay_rate, residue):
    channels, width = query_feat.shape
    heads, modes = decay_rate.shape
    hd = channels // heads
    heads_out = heads * n_tp // n_ctx
    group = 2 if heads_out % 2 == 0 else 1
    chunk = min(256, width)
    ng = heads // group
    ngo = heads_out // group
    part = hd // n_tp
    size = (n_ctx, n_tp, heads, hd, width, modes, chunk, group)
    vmem = pl.BlockSpec(memory_space=pltpu.VMEM)
    hbm = pl.BlockSpec(memory_space=pl.ANY)
    dma = pltpu.SemaphoreType.DMA
    return pl.pallas_call(
        functools.partial(kernel, size),
        out_shape=jax.ShapeDtypeStruct((heads_out, part, width * n_ctx), BF16),
        in_specs=[hbm, hbm, hbm, vmem, vmem, vmem, vmem],
        out_specs=hbm,
        scratch_shapes=[
            pltpu.VMEM((channels, width), BF16),
            pltpu.VMEM((channels, width), BF16),
            pltpu.VMEM((channels, width), BF16),
            pltpu.VMEM((16, channels), F32),
            pltpu.VMEM((3, channels, LANES), BF16),
            pltpu.VMEM((8, channels), F32),
            pltpu.VMEM((8, channels), F32),
            pltpu.VMEM((channels, width), BF16),
            pltpu.VMEM((channels, width), BF16),
            pltpu.VMEM((hd * width // chunk, chunk), F32),
            pltpu.VMEM((n_tp, heads, part, width), BF16),
            pltpu.VMEM((n_tp, heads, part, width), BF16),
            pltpu.VMEM((heads, modes, hd * width // chunk), F32),
            pltpu.VMEM((heads, modes, hd), F32),
            pltpu.VMEM((n_ctx, heads, modes, hd), F32),
            dma((3, ng)),
            dma((3,)),
            dma(()),
            dma(()),
            dma((ng, n_ctx)),
            dma((ng, n_ctx)),
            dma((n_tp, ng)),
            dma((n_tp, ng)),
            dma((n_tp, ng)),
            dma((n_ctx, ngo)),
        ],
        compiler_params=pltpu.CompilerParams(
            collective_id=0, has_side_effects=True, vmem_limit_bytes=50 * 1024 * 1024
        ),
        cost_estimate=pl.CostEstimate(
            flops=2 * channels * width * 1024, bytes_accessed=8 * channels * width, transcendentals=0
        ),
    )(
        query_feat, key_feat, value_feat, short_filter, skip[None], decay_rate, residue
    )


def solution(mesh):
    return jax.shard_map(
        functools.partial(per_device, mesh.shape["ctx"], mesh.shape["tp"]),
        mesh=mesh,
        in_specs=(
            P("tp", "ctx"),
            P("tp", "ctx"),
            P("tp", "ctx"),
            P(None, None, "tp"),
            P("tp"),
            P("tp", None),
            P("tp", None),
        ),
        out_specs=P("ctx", "tp", None),
        check_vma=False,
    )
```
